32 devices in a mesh: group: 4 (over y, x), key: 8 (over z, core).
Axes of the slice: x: 2, y: 2, z: 4, core: 2. Of those that a mesh axis runs over, the one named last changes fastest.
Arguments:
- src_desc: bfloat16 [8192, 256], P(('group', 'key'))
- tgt_desc: bfloat16 [16384, 256], P('key')
- src_weight: float32 [8192], P(('group', 'key')), may hold values from 0.05 to 20
- tgt_weight: float32 [16384], P('key'), may hold values from 0.05 to 20
- tgt_dual: float32 [16384], P('key'), may hold values from -1.2 to 1.2
- pair_blocks: int32 [4, 8, 2, 64], P('group', 'key'), may hold values from 0 to 7, as said below
- pair_count: int32 [4, 8], P('group', 'key'), may hold values from 8 to 64, as said below
Outputs:
- src_dual: float32 [8192], P(('group', 'key'))
- tgt_dual_new: float32 [16384], P('key')
The draws below stay inside these ranges and needn't reach their ends.
Inputs may be any that keep to these rules, and one draw needn't show every extreme that they name: `pair_blocks`: row 0 holds source clusters 0 to 7, row 1 target clusters 0 to 7; the live slots of one device are distinct pairs; every source cluster and every target cluster is in some live pair. `pair_count`: live slots come first.
All inputs are finite; a program needn't handle non-finite values.
Results may differ from the reference program's by a relative error of at most 0.0003.
Values may be sent and summed in bfloat16 or wider, within the bound.
A program may use at most 64 MiB of HBM per device.

```python
import math
import jax
import jax.numpy as jnp
from jax import lax

CLUSTER = 256
DESC = 256
TC_DEV = 8
SC_DEV = 1
PAIRS = 64
GROUPS = 4
KEYS = 8
SG = 8
NS = 8192
NT = 16384


def descriptor_draw(key, rows):
    return jax.random.normal(key, (rows, DESC), jnp.float32).astype(jnp.bfloat16)


def draw_src_desc(key, part):
    return descriptor_draw(jax.random.fold_in(key, 11), NS)


def draw_tgt_desc(key, part):
    return descriptor_draw(jax.random.fold_in(key, 13), NT)


def device_pairs(key, device):
    key_index = device % KEYS
    combos = SG * TC_DEV
    ranks = jax.random.permutation(jax.random.fold_in(key, device), combos).astype(jnp.int32)
    combo_ids = jnp.arange(combos, dtype=jnp.int32)
    src_ids = combo_ids // TC_DEV
    tgt_ids = combo_ids % TC_DEV
    anchor = src_ids == (key_index * SC_DEV + tgt_ids) % SG
    priority = jnp.where(anchor, tgt_ids - combos, ranks)
    order = jnp.argsort(priority, stable=True)[:PAIRS].astype(jnp.int32)
    return jnp.stack([order // TC_DEV, order % TC_DEV], axis=0)


def draw_pair_blocks(key, part):
    base = jax.random.fold_in(key, 17)
    devices_all = jnp.arange(GROUPS * KEYS, dtype=jnp.int32)
    lists = jax.vmap(lambda device: device_pairs(base, device))(devices_all)
    return lists.reshape(GROUPS, KEYS, 2, PAIRS).astype(jnp.int32)


def draw_pair_count(key, part):
    base = jax.random.fold_in(key, 19)
    total = GROUPS * KEYS
    draws = jax.random.randint(base, (total,), 0, 1024, jnp.int32)
    counts = TC_DEV + (PAIRS - TC_DEV) * draws * draws // (1023 * 1023)
    busiest = jax.random.randint(jax.random.fold_in(base, 3), (), 0, total, jnp.int32)
    counts = counts.at[busiest].set(PAIRS)
    counts = counts.at[(busiest + 1) % total].set(TC_DEV)
    return counts.reshape(GROUPS, KEYS).astype(jnp.int32)


def block_levels(key, dims, pieces, least, top_value):
    gain = 1.0
    for dim, shards_of in pieces:
        steps = jax.random.uniform(jax.random.fold_in(jax.random.fold_in(key, 6), dim), (shards_of,), jnp.float32, least / len(pieces), top_value / len(pieces))
        gain = gain * jnp.repeat(jnp.exp(steps), dims[dim] // shards_of).reshape((-1,) + (1,) * (len(dims) - 1 - dim))
    return gain


def gaussian(stream_key, shape, spread, most, cuts=(), kind=jnp.bfloat16):
    level = block_levels(stream_key, shape, cuts, -0.22, 0.18) if cuts else 1.0
    array = jax.random.normal(stream_key, shape, jnp.float32) * spread * level
    return jnp.minimum(jnp.maximum(array, -most), most).astype(kind)


def setup_inputs(seed: int = 0) -> dict:
    keys = jax.random.split(jax.random.key(seed), 8)
    src_desc = draw_src_desc(jax.random.fold_in(keys[7], 71), 0)
    tgt_desc = draw_tgt_desc(jax.random.fold_in(keys[7], 71), 0)
    src_weight = jnp.clip(jnp.exp(math.log(20.0) - 5.9914645 * jax.random.uniform(keys[2], (NS,), jnp.float32) ** block_levels(keys[2], (NS,), ((0, 32),), -0.2, 0.2)), 0.05, 20.0)
    tgt_weight = jnp.clip(jnp.exp(math.log(20.0) - 5.9914645 * jax.random.uniform(keys[3], (NT,), jnp.float32) ** block_levels(keys[3], (NT,), ((0, 8),), -0.2, 0.2)), 0.05, 20.0)
    tgt_dual = gaussian(keys[4], (NT,), 0.2, 1.2, ((0, 8),), jnp.float32)
    pair_blocks = draw_pair_blocks(jax.random.fold_in(keys[7], 71), 0)
    pair_count = draw_pair_count(jax.random.fold_in(keys[7], 71), 0)
    return dict(src_desc=src_desc, tgt_desc=tgt_desc, src_weight=src_weight, tgt_weight=tgt_weight, tgt_dual=tgt_dual, pair_blocks=pair_blocks, pair_count=pair_count)


ENTROPY = 0.05


def reference(src_desc, tgt_desc, src_weight, tgt_weight, tgt_dual, pair_blocks, pair_count):
    sq_src = jnp.sum(src_desc.astype(jnp.float32) ** 2, axis=1) / DESC
    sq_tgt = jnp.sum(tgt_desc.astype(jnp.float32) ** 2, axis=1) / DESC
    devices_all = GROUPS * KEYS
    blocks = pair_blocks.reshape(devices_all, 2, PAIRS)
    counts = pair_count.reshape(devices_all)
    device_ids = jnp.arange(devices_all, dtype=jnp.int32)
    group_ids = device_ids // KEYS
    key_ids = device_ids % KEYS
    src_glob = (group_ids[:, None] * SG + blocks[:, 0, :]).reshape(-1).astype(jnp.int32)
    tgt_glob = (key_ids[:, None] * TC_DEV + blocks[:, 1, :]).reshape(-1).astype(jnp.int32)
    live = (jnp.arange(PAIRS, dtype=jnp.int32)[None, :] < counts[:, None]).reshape(-1)

    def block_cost(src_id, tgt_id):
        src_rows = lax.dynamic_slice_in_dim(src_desc, src_id * CLUSTER, CLUSTER, 0)
        tgt_rows = lax.dynamic_slice_in_dim(tgt_desc, tgt_id * CLUSTER, CLUSTER, 0)
        inner = lax.dot_general(src_rows, tgt_rows, (((1,), (1,)), ((), ())), preferred_element_type=jnp.float32)
        src_sq = lax.dynamic_slice_in_dim(sq_src, src_id * CLUSTER, CLUSTER, 0)
        tgt_sq = lax.dynamic_slice_in_dim(sq_tgt, tgt_id * CLUSTER, CLUSTER, 0)
        return src_sq[:, None] + tgt_sq[None, :] - (2.0 / DESC) * inner

    def first_sweep(carry, item):
        src_id, tgt_id, alive = item
        cost = block_cost(src_id, tgt_id)
        tgt_pot = lax.dynamic_slice_in_dim(tgt_dual, tgt_id * CLUSTER, CLUSTER, 0)
        rows_lse = jax.nn.logsumexp((tgt_pot[None, :] - cost) / ENTROPY, axis=1)
        rows_lse = jnp.where(alive, rows_lse, jnp.float32(-jnp.inf))
        old = lax.dynamic_index_in_dim(carry, src_id, 0, keepdims=False)
        return lax.dynamic_update_index_in_dim(carry, jnp.logaddexp(old, rows_lse), src_id, 0), None

    lse_src = jnp.full((NS // CLUSTER, CLUSTER), -jnp.inf, jnp.float32)
    lse_src, _ = lax.scan(first_sweep, lse_src, (src_glob, tgt_glob, live))
    src_dual = ENTROPY * jnp.log(src_weight) - ENTROPY * lse_src.reshape(-1)

    def second_sweep(carry, item):
        src_id, tgt_id, alive = item
        cost = block_cost(src_id, tgt_id)
        src_pot = lax.dynamic_slice_in_dim(src_dual, src_id * CLUSTER, CLUSTER, 0)
        cols_lse = jax.nn.logsumexp((src_pot[:, None] - cost) / ENTROPY, axis=0)
        cols_lse = jnp.where(alive, cols_lse, jnp.float32(-jnp.inf))
        old = lax.dynamic_index_in_dim(carry, tgt_id, 0, keepdims=False)
        return lax.dynamic_update_index_in_dim(carry, jnp.logaddexp(old, cols_lse), tgt_id, 0), None

    lse_tgt = jnp.full((NT // CLUSTER, CLUSTER), -jnp.inf, jnp.float32)
    lse_tgt, _ = lax.scan(second_sweep, lse_tgt, (src_glob, tgt_glob, live))
    tgt_dual_new = ENTROPY * jnp.log(tgt_weight) - ENTROPY * lse_tgt.reshape(-1)
    return (src_dual, tgt_dual_new)
```

```python
import functools
import math

import jax
import jax.numpy as jnp
from jax import lax
from jax.experimental import pallas as pl
from jax.experimental.pallas import tpu as pltpu
from jax.sharding import PartitionSpec as P

CLUSTER = 256
HALF = 128
ENTROPY = 0.05
NEG_FLOOR = -1e30
LOG2E = 1.0 / math.log(2.0)
TO_BASE2 = LOG2E / ENTROPY
FROM_BASE2 = ENTROPY / LOG2E
MESH = pl.DeviceIdType.MESH
NT = (((1,), (1,)), ((), ()))


def nt_dot(a, b):
    return lax.dot_general(a, b, NT, preferred_element_type=jnp.float32)


def square_row(rows):
    wide = rows.astype(jnp.float32)
    square = wide * wide
    high = square.astype(jnp.bfloat16)
    low = (square - high.astype(jnp.float32)).astype(jnp.bfloat16)
    ones = jnp.ones((8, rows.shape[1]), jnp.bfloat16)
    return (nt_dot(ones, high) + nt_dot(ones, low))[0:1] * (1.0 / rows.shape[1])


def spread(row):
    return jnp.broadcast_to(row, (HALF, HALF)).T


def block_sums(left, right, scale, offset_ref, start):
    inner = nt_dot(left, right) * scale
    offset = offset_ref[pl.ds(start, CLUSTER), :]
    tops, totals = [], []
    for half in range(CLUSTER // HALF):
        score = inner[:, half * HALF : (half + 1) * HALF] + offset
        top = jnp.max(score, axis=0, keepdims=True)
        totals.append(jnp.sum(jnp.exp2(score - top), axis=0, keepdims=True))
        tops.append(top)
    return jnp.concatenate(tops, axis=1), jnp.concatenate(totals, axis=1)


def merge(tops, totals, listed):
    tops = jnp.where(listed, tops, NEG_FLOOR)
    best = jnp.max(tops, axis=0, keepdims=True)
    total = jnp.sum(jnp.where(listed, totals * jnp.exp2(tops - best), 0.0), axis=0, keepdims=True)
    return best + jnp.log(total) * LOG2E


def kernel(groups, keys, src_ref, tgt_ref, sw_ref, tw_ref, td_ref, pb_ref, pc_ref, so_ref, to_ref,
           gs, plse, wg, tl, acol, bcol, brow, sqt, mt, lt,
           s_send, s_recv, p_send, p_recv, w_send, w_recv, t_send, t_recv):
    g, k = lax.axis_index("group"), lax.axis_index("key")
    pos, core = k // 2, k % 2
    n_pos = keys // 2
    width = src_ref.shape[1]
    n_tgt = tgt_ref.shape[0] // CLUSTER
    scale = 2.0 / width * TO_BASE2

    def key_peer(r):
        return lax.rem(k + r, keys)

    barrier = pltpu.get_barrier_semaphore()

    def greet(r, carry):
        pl.semaphore_signal(barrier, inc=1, device_id=(g, key_peer(r)), device_id_type=MESH)
        return carry

    lax.fori_loop(1, keys, greet, 0)
    for r in range(1, groups):
        pl.semaphore_signal(barrier, inc=1, device_id=(lax.rem(g + r, groups), k), device_id_type=MESH)
    gs[k] = src_ref[...]
    wg[k] = jnp.log(jnp.concatenate([sw_ref[0:1, :], sw_ref[1:2, :]], axis=1)) * LOG2E
    pl.semaphore_wait(barrier, keys + groups - 2)

    def shard(slot, lane):
        target = (2 * (pos - 1) + core, 2 * (pos + 1) + core, 2 * pos + 1 - core)[lane]
        return pltpu.make_async_remote_copy(
            src_ref=gs.at[slot], dst_ref=gs.at[slot], send_sem=s_send.at[lane, slot],
            recv_sem=s_recv.at[slot], device_id=(g, target), device_id_type=MESH)

    def weights(r):
        return pltpu.make_async_remote_copy(
            src_ref=wg.at[k], dst_ref=wg.at[k], send_sem=w_send.at[r], recv_sem=w_recv.at[k],
            device_id=(g, key_peer(r)), device_id_type=MESH)

    def weights_from(r):
        peer = key_peer(r)
        return pltpu.make_async_remote_copy(
            src_ref=wg.at[peer], dst_ref=wg.at[peer], send_sem=w_send.at[r], recv_sem=w_recv.at[peer],
            device_id=(g, peer), device_id_type=MESH)

    @pl.when(pos > 0)
    def _():
        shard(k, 0).start()

    @pl.when(pos < n_pos - 1)
    def _():
        shard(k, 1).start()

    shard(k, 2).start()

    def send_weights(r, carry):
        weights(r).start()
        return carry

    lax.fori_loop(1, keys, send_weights, 0)

    def prepare(t, carry):
        sq = square_row(tgt_ref[pl.ds(pl.multiple_of(t * CLUSTER, CLUSTER), CLUSTER), :])
        sqt[pl.ds(t, 1), :] = sq
        for half in range(2):
            row = (td_ref[pl.ds(2 * t + half, 1), :] - sq[:, half * HALF : (half + 1) * HALF]) * TO_BASE2
            acol[pl.ds(pl.multiple_of(t * CLUSTER + half * HALF, HALF), HALF), :] = spread(row)
        return carry

    lax.fori_loop(0, n_tgt, prepare, 0)

    slots = pb_ref.shape[1]
    live = lax.broadcasted_iota(jnp.int32, (1, slots), 1) < pc_ref[...]
    src_ids = jnp.where(live, pb_ref[0:1, :], -1)
    tgt_ids = pb_ref[1:2, :]

    def listed_rows(rows, row_ids, other_ids, other):
        hit = (lax.broadcasted_iota(jnp.int32, (rows, slots), 0) == row_ids) & (other_ids == other)
        return jnp.sum(jnp.where(hit, 1.0, 0.0), axis=1, keepdims=True) > 0.0

    def first(slot):
        src = gs[slot]
        for t in range(n_tgt):
            top, total = block_sums(tgt_ref[t * CLUSTER : (t + 1) * CLUSTER, :], src, scale, acol, t * CLUSTER)
            mt[t : t + 1, :] = top
            lt[t : t + 1, :] = total
        listed = listed_rows(n_tgt, tgt_ids, src_ids, slot)
        plse[k, pl.ds(slot, 1), :] = merge(mt[0:n_tgt, :], lt[0:n_tgt, :], listed)

    def distance(d, carry):
        before, after = pos - d, pos + d

        @pl.when((d > 0) & (before >= 0))
        def _():
            slot = 2 * before + core
            shard(slot, 1).wait_recv()

            @pl.when(pos < n_pos - 1)
            def _():
                shard(slot, 1).start()

            shard(slot, 2).start()

        @pl.when((d > 0) & (after < n_pos))
        def _():
            slot = 2 * after + core
            shard(slot, 0).wait_recv()

            @pl.when(pos > 0)
            def _():
                shard(slot, 0).start()

            shard(slot, 2).start()

        def job(w, carry):
            forward, other = w % 2, w // 2
            at = pos + d * (2 * forward - 1)

            @pl.when((at >= 0) & (at < n_pos) & ((d > 0) | (forward == 0)))
            def _():
                slot = 2 * at + core + other * (1 - 2 * core)

                @pl.when(other == 1)
                def _():
                    shard(slot, 2).wait_recv()

                first(slot)

            return carry

        return lax.fori_loop(0, 4, job, carry)

    lax.fori_loop(0, n_pos, distance, 0)

    def partial(r):
        return pltpu.make_async_remote_copy(
            src_ref=plse.at[k], dst_ref=plse.at[k], send_sem=p_send.at[r], recv_sem=p_recv.at[k],
            device_id=(g, key_peer(r)), device_id_type=MESH)

    def partial_from(r):
        peer = key_peer(r)
        return pltpu.make_async_remote_copy(
            src_ref=plse.at[peer], dst_ref=plse.at[peer], send_sem=p_send.at[r], recv_sem=p_recv.at[peer],
            device_id=(g, peer), device_id_type=MESH)

    def send_partial(r, carry):
        partial(r).start()
        return carry

    def take_partial(r, carry):
        weights_from(r).wait_recv()
        partial_from(r).wait_recv()
        return carry

    lax.fori_loop(1, keys, send_partial, 0)
    own_sq = square_row(src_ref[...])
    lax.fori_loop(1, keys, take_partial, 0)

    every = plse[...]
    best = jnp.max(every, axis=0)
    total = jnp.sum(jnp.exp2(every - best[None]), axis=0)
    brow[...] = wg[...].reshape(keys, CLUSTER) - (best + jnp.log(total) * LOG2E)
    own = brow[pl.ds(k, 1), :] * FROM_BASE2 + own_sq
    so_ref[0:1, :] = own[:, :HALF]
    so_ref[1:2, :] = own[:, HALF:]

    def columns(s, carry):
        row = brow[pl.ds(s, 1), :]
        for half in range(2):
            bcol[pl.ds(pl.multiple_of(s * CLUSTER + half * HALF, HALF), HALF), :] = spread(
                row[:, half * HALF : (half + 1) * HALF])
        return carry

    lax.fori_loop(0, keys, columns, 0)

    step = math.gcd(keys, 8)

    def second(t, carry):
        tgt = tgt_ref[pl.ds(pl.multiple_of(t * CLUSTER, CLUSTER), CLUSTER), :]

        def some(c, carry):
            for j in range(step):
                s = c * step + j
                top, total = block_sums(gs[s], tgt, scale, bcol, pl.multiple_of(s * CLUSTER, CLUSTER))
                mt[pl.ds(s, 1), :] = top
                lt[pl.ds(s, 1), :] = total
            return carry

        lax.fori_loop(0, keys // step, some, 0)
        listed = listed_rows(keys, src_ids, tgt_ids, t)
        tl[g, pl.ds(t, 1), :] = merge(mt[0:keys, :], lt[0:keys, :], listed)
        return carry

    lax.fori_loop(0, n_tgt, second, 0)

    def column(r):
        return pltpu.make_async_remote_copy(
            src_ref=tl.at[g], dst_ref=tl.at[g], send_sem=t_send.at[r], recv_sem=t_recv.at[g],
            device_id=(lax.rem(g + r, groups), k), device_id_type=MESH)

    def column_from(r):
        peer = lax.rem(g + r, groups)
        return pltpu.make_async_remote_copy(
            src_ref=tl.at[peer], dst_ref=tl.at[peer], send_sem=t_send.at[r], recv_sem=t_recv.at[peer],
            device_id=(peer, k), device_id_type=MESH)

    for r in range(1, groups):
        column(r).start()

    def sent_shards(p, carry):
        slot = 2 * p + core

        @pl.when((pos > 0) & (p >= pos))
        def _():
            shard(slot, 0).wait_send()

        @pl.when((pos < n_pos - 1) & (p <= pos))
        def _():
            shard(slot, 1).wait_send()

        shard(slot, 2).wait_send()
        return carry

    def sent_rows(r, carry):
        weights(r).wait_send()
        partial(r).wait_send()
        return carry

    lax.fori_loop(0, n_pos, sent_shards, 0)
    lax.fori_loop(1, keys, sent_rows, 0)
    for r in range(1, groups):
        column_from(r).wait_recv()

    every = tl[...]
    best = jnp.max(every, axis=0)
    total = jnp.sum(jnp.exp2(every - best[None]), axis=0)
    lse = best + jnp.log(total) * LOG2E
    new = sqt[...] - lse * FROM_BASE2
    for t in range(n_tgt):
        for half in range(2):
            at = 2 * t + half
            to_ref[at : at + 1, :] = (
                new[t : t + 1, half * HALF : (half + 1) * HALF] + jnp.log(tw_ref[at : at + 1, :]) * ENTROPY)
    for r in range(1, groups):
        column(r).wait_send()


def local(groups, keys, src_desc, tgt_desc, src_weight, tgt_weight, tgt_dual, pair_blocks, pair_count):
    rows, width = tgt_desc.shape
    n_tgt = rows // CLUSTER
    slots = pair_blocks.shape[3]
    f32 = jnp.float32
    dma = pltpu.SemaphoreType.DMA
    most = max(keys, n_tgt)
    blocks = 2 * keys * n_tgt
    src_dual, tgt_new = pl.pallas_call(
        functools.partial(kernel, groups, keys),
        out_shape=(jax.ShapeDtypeStruct((CLUSTER // HALF, HALF), f32),
                   jax.ShapeDtypeStruct((rows // HALF, HALF), f32)),
        in_specs=[pl.BlockSpec(memory_space=pltpu.VMEM)] * 7,
        out_specs=[pl.BlockSpec(memory_space=pltpu.VMEM)] * 2,
        scratch_shapes=[
            pltpu.VMEM((keys, CLUSTER, width), jnp.bfloat16),
            pltpu.VMEM((keys, keys, CLUSTER), f32),
            pltpu.VMEM((keys, 1, CLUSTER), f32),
            pltpu.VMEM((groups, n_tgt, CLUSTER), f32),
            pltpu.VMEM((rows, HALF), f32),
            pltpu.VMEM((keys * CLUSTER, HALF), f32),
            pltpu.VMEM((keys, CLUSTER), f32),
            pltpu.VMEM((n_tgt, CLUSTER), f32),
            pltpu.VMEM((most, CLUSTER), f32),
            pltpu.VMEM((most, CLUSTER), f32),
            dma((3, keys)), dma((keys,)),
            dma((keys,)), dma((keys,)),
            dma((keys,)), dma((keys,)),
            dma((groups,)), dma((groups,)),
        ],
        compiler_params=pltpu.CompilerParams(
            collective_id=0, has_side_effects=True, vmem_limit_bytes=44 * 1024 * 1024),
        cost_estimate=pl.CostEstimate(
            flops=blocks * 2 * CLUSTER * CLUSTER * width, bytes_accessed=2 * rows * width,
            transcendentals=blocks * CLUSTER * CLUSTER),
    )(
        src_desc, tgt_desc,
        src_weight.reshape(CLUSTER // HALF, HALF),
        tgt_weight.reshape(rows // HALF, HALF),
        tgt_dual.reshape(rows // HALF, HALF),
        pair_blocks.reshape(2, slots), pair_count.reshape(1, 1),
    )
    return src_dual.reshape(CLUSTER), tgt_new.reshape(rows)


def solution(mesh):
    groups, keys = mesh.shape["group"], mesh.shape["key"]
    in_specs = (
        P(("group", "key"), None),
        P("key", None),
        P(("group", "key")),
        P("key"),
        P("key"),
        P("group", "key", None, None),
        P("group", "key"),
    )
    out_specs = (P(("group", "key")), P("key"))
    return jax.shard_map(functools.partial(local, groups, keys), mesh=mesh, in_specs=in_specs,
                         out_specs=out_specs, check_vma=False)
```

```python
import functools
import math

import jax
import jax.numpy as jnp
from jax import lax
from jax.experimental import pallas as pl
from jax.experimental.pallas import tpu as pltpu
from jax.sharding import PartitionSpec as P

CLUSTER = 256
HALF = 128
ENTROPY = 0.05
NEG_FLOOR = -1e30
LOG2E = 1.0 / math.log(2.0)
TO_BASE2 = LOG2E / ENTROPY
FROM_BASE2 = ENTROPY / LOG2E
MESH = pl.DeviceIdType.MESH
NT = (((1,), (1,)), ((), ()))


def nt_dot(a, b):
    return lax.dot_general(a, b, NT, preferred_element_type=jnp.float32)


def square_row(rows):
    wide = rows.astype(jnp.float32)
    square = wide * wide
    high = square.astype(jnp.bfloat16)
    low = (square - high.astype(jnp.float32)).astype(jnp.bfloat16)
    ones = jnp.ones((8, rows.shape[1]), jnp.bfloat16)
    return (nt_dot(ones, high) + nt_dot(ones, low))[0:1] * (1.0 / rows.shape[1])


def spread(row):
    return jnp.broadcast_to(row, (HALF, HALF)).T


def block_sums(left, right, scale, offset_ref, start):
    inner = nt_dot(left, right) * scale
    offset = offset_ref[pl.ds(start, CLUSTER), :]
    tops, totals = [], []
    for half in range(CLUSTER // HALF):
        score = inner[:, half * HALF : (half + 1) * HALF] + offset
        top = jnp.max(score, axis=0, keepdims=True)
        totals.append(jnp.sum(jnp.exp2(score - top), axis=0, keepdims=True))
        tops.append(top)
    return jnp.concatenate(tops, axis=1), jnp.concatenate(totals, axis=1)


def merge(tops, totals, listed):
    tops = jnp.where(listed, tops, NEG_FLOOR)
    best = jnp.max(tops, axis=0, keepdims=True)
    total = jnp.sum(jnp.where(listed, totals * jnp.exp2(tops - best), 0.0), axis=0, keepdims=True)
    return best + jnp.log(total) * LOG2E


def kernel(groups, keys, src_hbm, tgt_hbm, sw_hbm, tw_hbm, td_hbm, pb_hbm, pc_ref, so_ref, to_ref,
           tgt_ref, sw_ref, tw_ref, td_ref, pb_ref, load_sem, gs, plse, wg, tl, acol, bcol, brow, sqt, mt, lt,
           s_send, s_recv, p_send, p_recv, w_send, w_recv, t_send, t_recv):
    g, k = lax.axis_index("group"), lax.axis_index("key")
    pos, core = k // 2, k % 2
    n_pos = keys // 2
    width = tgt_ref.shape[1]
    n_tgt = tgt_ref.shape[0] // CLUSTER
    scale = 2.0 / width * TO_BASE2

    def key_peer(r):
        return lax.rem(k + r, keys)

    pairs = ((src_hbm, gs.at[k]), (sw_hbm, sw_ref), (tgt_hbm, tgt_ref), (td_hbm, td_ref),
             (pb_hbm, pb_ref), (tw_hbm, tw_ref))
    loads = [pltpu.make_async_copy(a, b, load_sem.at[n]) for n, (a, b) in enumerate(pairs)]
    for load in loads:
        load.start()

    barrier = pltpu.get_barrier_semaphore()

    def greet(r, carry):
        pl.semaphore_signal(barrier, inc=1, device_id=(g, key_peer(r)), device_id_type=MESH)
        return carry

    lax.fori_loop(1, keys, greet, 0)
    for r in range(1, groups):
        pl.semaphore_signal(barrier, inc=1, device_id=(lax.rem(g + r, groups), k), device_id_type=MESH)
    loads[0].wait()
    loads[1].wait()
    wg[k] = jnp.log(jnp.concatenate([sw_ref[0:1, :], sw_ref[1:2, :]], axis=1)) * LOG2E
    pl.semaphore_wait(barrier, keys + groups - 2)

    def shard(slot, lane, part):
        target = (2 * (pos - 1) + core, 2 * (pos + 1) + core, 2 * pos + 1 - core)[lane]
        piece = gs.at[slot, pl.ds(pl.multiple_of(part * HALF, HALF), HALF)]
        return pltpu.make_async_remote_copy(
            src_ref=piece, dst_ref=piece, send_sem=s_send.at[lane, slot, part],
            recv_sem=s_recv.at[slot, part], device_id=(g, target), device_id_type=MESH)

    def weights(r):
        return pltpu.make_async_remote_copy(
            src_ref=wg.at[k], dst_ref=wg.at[k], send_sem=w_send.at[r], recv_sem=w_recv.at[k],
            device_id=(g, key_peer(r)), device_id_type=MESH)

    def weights_from(r):
        peer = key_peer(r)
        return pltpu.make_async_remote_copy(
            src_ref=wg.at[peer], dst_ref=wg.at[peer], send_sem=w_send.at[r], recv_sem=w_recv.at[peer],
            device_id=(g, peer), device_id_type=MESH)

    def send_own(part, carry):
        @pl.when(pos > 0)
        def _():
            shard(k, 0, part).start()

        @pl.when(pos < n_pos - 1)
        def _():
            shard(k, 1, part).start()

        shard(k, 2, part).start()
        return carry

    lax.fori_loop(0, 2, send_own, 0)

    def send_weights(r, carry):
        weights(r).start()
        return carry

    lax.fori_loop(1, keys, send_weights, 0)

    for load in loads[2:]:
        load.wait()

    def prepare(t, carry):
        sq = square_row(tgt_ref[pl.ds(pl.multiple_of(t * CLUSTER, CLUSTER), CLUSTER), :])
        sqt[pl.ds(t, 1), :] = sq
        for half in range(2):
            row = (td_ref[pl.ds(2 * t + half, 1), :] - sq[:, half * HALF : (half + 1) * HALF]) * TO_BASE2
            acol[pl.ds(pl.multiple_of(t * CLUSTER + half * HALF, HALF), HALF), :] = spread(row)
        return carry

    lax.fori_loop(0, n_tgt, prepare, 0)

    slots = pb_ref.shape[1]
    live = lax.broadcasted_iota(jnp.int32, (1, slots), 1) < pc_ref[...]
    src_ids = jnp.where(live, pb_ref[0:1, :], -1)
    tgt_ids = pb_ref[1:2, :]

    def listed_rows(rows, row_ids, other_ids, other):
        hit = (lax.broadcasted_iota(jnp.int32, (rows, slots), 0) == row_ids) & (other_ids == other)
        return jnp.sum(jnp.where(hit, 1.0, 0.0), axis=1, keepdims=True) > 0.0

    def first(slot):
        src = gs[slot]
        for t in range(n_tgt):
            top, total = block_sums(tgt_ref[t * CLUSTER : (t + 1) * CLUSTER, :], src, scale, acol, t * CLUSTER)
            mt[t : t + 1, :] = top
            lt[t : t + 1, :] = total
        listed = listed_rows(n_tgt, tgt_ids, src_ids, slot)
        plse[k, pl.ds(slot, 1), :] = merge(mt[0:n_tgt, :], lt[0:n_tgt, :], listed)

    def stage(n, carry):
        d, part = n // 2, n % 2
        before, after = pos - d, pos + d

        @pl.when((d > 0) & (before >= 0))
        def _():
            slot = 2 * before + core
            shard(slot, 1, part).wait_recv()

            @pl.when(pos < n_pos - 1)
            def _():
                shard(slot, 1, part).start()

            shard(slot, 2, part).start()

        @pl.when((d > 0) & (after < n_pos))
        def _():
            slot = 2 * after + core
            shard(slot, 0, part).wait_recv()

            @pl.when(pos > 0)
            def _():
                shard(slot, 0, part).start()

            shard(slot, 2, part).start()

        far = d - 1 + part

        def job(forward, carry):
            at = pos + far * (2 * forward - 1)

            @pl.when((at >= 0) & (at < n_pos) & (far >= forward))
            def _():
                slot = 2 * at + core + (1 - part) * (1 - 2 * core)

                @pl.when(part == 0)
                def _():
                    shard(slot, 2, 0).wait_recv()
                    shard(slot, 2, 1).wait_recv()

                first(slot)

            return carry

        return lax.fori_loop(0, 2, job, carry)

    lax.fori_loop(1, 2 * n_pos + 1, stage, 0)

    def partial(r):
        return pltpu.make_async_remote_copy(
            src_ref=plse.at[k], dst_ref=plse.at[k], send_sem=p_send.at[r], recv_sem=p_recv.at[k],
            device_id=(g, key_peer(r)), device_id_type=MESH)

    def partial_from(r):
        peer = key_peer(r)
        return pltpu.make_async_remote_copy(
            src_ref=plse.at[peer], dst_ref=plse.at[peer], send_sem=p_send.at[r], recv_sem=p_recv.at[peer],
            device_id=(g, peer), device_id_type=MESH)

    def send_partial(r, carry):
        partial(r).start()
        return carry

    def take_partial(r, carry):
        weights_from(r).wait_recv()
        partial_from(r).wait_recv()
        return carry

    lax.fori_loop(1, keys, send_partial, 0)
    own_sq = square_row(gs[k])
    lax.fori_loop(1, keys, take_partial, 0)

    every = plse[...]
    best = jnp.max(every, axis=0)
    total = jnp.sum(jnp.exp2(every - best[None]), axis=0)
    brow[...] = wg[...].reshape(keys, CLUSTER) - (best + jnp.log(total) * LOG2E)
    own = brow[pl.ds(k, 1), :] * FROM_BASE2 + own_sq
    so_ref[0:1, :] = own[:, :HALF]
    so_ref[1:2, :] = own[:, HALF:]

    def columns(s, carry):
        row = brow[pl.ds(s, 1), :]
        for half in range(2):
            bcol[pl.ds(pl.multiple_of(s * CLUSTER + half * HALF, HALF), HALF), :] = spread(
                row[:, half * HALF : (half + 1) * HALF])
        return carry

    lax.fori_loop(0, keys, columns, 0)

    step = math.gcd(keys, 8)

    def second(t, carry):
        tgt = tgt_ref[pl.ds(pl.multiple_of(t * CLUSTER, CLUSTER), CLUSTER), :]

        def some(c, carry):
            for j in range(step):
                s = c * step + j
                top, total = block_sums(gs[s], tgt, scale, bcol, pl.multiple_of(s * CLUSTER, CLUSTER))
                mt[pl.ds(s, 1), :] = top
                lt[pl.ds(s, 1), :] = total
            return carry

        lax.fori_loop(0, keys // step, some, 0)
        listed = listed_rows(keys, src_ids, tgt_ids, t)
        tl[g, pl.ds(t, 1), :] = merge(mt[0:keys, :], lt[0:keys, :], listed)
        return carry

    lax.fori_loop(0, n_tgt, second, 0, unroll=2)

    def column(r):
        return pltpu.make_async_remote_copy(
            src_ref=tl.at[g], dst_ref=tl.at[g], send_sem=t_send.at[r], recv_sem=t_recv.at[g],
            device_id=(lax.rem(g + r, groups), k), device_id_type=MESH)

    def column_from(r):
        peer = lax.rem(g + r, groups)
        return pltpu.make_async_remote_copy(
            src_ref=tl.at[peer], dst_ref=tl.at[peer], send_sem=t_send.at[r], recv_sem=t_recv.at[peer],
            device_id=(peer, k), device_id_type=MESH)

    for r in range(1, groups):
        column(r).start()

    def sent_shards(p, carry):
        slot = 2 * p + core
        for part in range(2):

            @pl.when((pos > 0) & (p >= pos))
            def _():
                shard(slot, 0, part).wait_send()

            @pl.when((pos < n_pos - 1) & (p <= pos))
            def _():
                shard(slot, 1, part).wait_send()

            shard(slot, 2, part).wait_send()
        return carry

    def sent_rows(r, carry):
        weights(r).wait_send()
        partial(r).wait_send()
        return carry

    lax.fori_loop(0, n_pos, sent_shards, 0)
    lax.fori_loop(1, keys, sent_rows, 0)
    for r in range(1, groups):
        column_from(r).wait_recv()

    every = tl[...]
    best = jnp.max(every, axis=0)
    total = jnp.sum(jnp.exp2(every - best[None]), axis=0)
    lse = best + jnp.log(total) * LOG2E
    new = sqt[...] - lse * FROM_BASE2
    for t in range(n_tgt):
        for half in range(2):
            at = 2 * t + half
            to_ref[at : at + 1, :] = (
                new[t : t + 1, half * HALF : (half + 1) * HALF] + jnp.log(tw_ref[at : at + 1, :]) * ENTROPY)
    for r in range(1, groups):
        column(r).wait_send()


def local(groups, keys, src_desc, tgt_desc, src_weight, tgt_weight, tgt_dual, pair_blocks, pair_count):
    rows, width = tgt_desc.shape
    n_tgt = rows // CLUSTER
    slots = pair_blocks.shape[3]
    f32 = jnp.float32
    dma = pltpu.SemaphoreType.DMA
    most = max(keys, n_tgt)
    blocks = 2 * keys * n_tgt
    src_dual, tgt_new = pl.pallas_call(
        functools.partial(kernel, groups, keys),
        out_shape=(jax.ShapeDtypeStruct((CLUSTER // HALF, HALF), f32),
                   jax.ShapeDtypeStruct((rows // HALF, HALF), f32)),
        in_specs=[pl.BlockSpec(memory_space=pltpu.HBM)] * 6 + [pl.BlockSpec(memory_space=pltpu.VMEM)],
        out_specs=[pl.BlockSpec(memory_space=pltpu.VMEM)] * 2,
        scratch_shapes=[
            pltpu.VMEM((rows, width), jnp.bfloat16),
            pltpu.VMEM((CLUSTER // HALF, HALF), f32),
            pltpu.VMEM((rows // HALF, HALF), f32),
            pltpu.VMEM((rows // HALF, HALF), f32),
            pltpu.VMEM((2, slots), jnp.int32),
            dma((6,)),
            pltpu.VMEM((keys, CLUSTER, width), jnp.bfloat16),
            pltpu.VMEM((keys, keys, CLUSTER), f32),
            pltpu.VMEM((keys, 1, CLUSTER), f32),
            pltpu.VMEM((groups, n_tgt, CLUSTER), f32),
            pltpu.VMEM((rows, HALF), f32),
            pltpu.VMEM((keys * CLUSTER, HALF), f32),
            pltpu.VMEM((keys, CLUSTER), f32),
            pltpu.VMEM((n_tgt, CLUSTER), f32),
            pltpu.VMEM((most, CLUSTER), f32),
            pltpu.VMEM((most, CLUSTER), f32),
            dma((3, keys, 2)), dma((keys, 2)),
            dma((keys,)), dma((keys,)),
            dma((keys,)), dma((keys,)),
            dma((groups,)), dma((groups,)),
        ],
        compiler_params=pltpu.CompilerParams(
            collective_id=0, has_side_effects=True, vmem_limit_bytes=63 * 1024 * 1024),
        cost_estimate=pl.CostEstimate(
            flops=blocks * 2 * CLUSTER * CLUSTER * width, bytes_accessed=2 * rows * width,
            transcendentals=blocks * CLUSTER * CLUSTER),
    )(
        src_desc, tgt_desc,
        src_weight.reshape(CLUSTER // HALF, HALF),
        tgt_weight.reshape(rows // HALF, HALF),
        tgt_dual.reshape(rows // HALF, HALF),
        pair_blocks.reshape(2, slots), pair_count.reshape(1, 1),
    )
    return src_dual.reshape(CLUSTER), tgt_new.reshape(rows)


def solution(mesh):
    groups, keys = mesh.shape["group"], mesh.shape["key"]
    in_specs = (
        P(("group", "key"), None),
        P("key", None),
        P(("group", "key")),
        P("key"),
        P("key"),
        P("group", "key", None, None),
        P("group", "key"),
    )
    out_specs = (P(("group", "key")), P("key"))
    return jax.shard_map(functools.partial(local, groups, keys), mesh=mesh, in_specs=in_specs,
                         out_specs=out_specs, check_vma=False)
```

```python
import functools
import math

import jax
import jax.numpy as jnp
from jax import lax
from jax.experimental import pallas as pl
from jax.experimental.pallas import tpu as pltpu
from jax.sharding import PartitionSpec as P

CLUSTER = 256
HALF = 128
ENTROPY = 0.05
NEG_FLOOR = -1e30
LANES = 8
CHUNK = 128
PARTS = CLUSTER // CHUNK * LANES
MESH = pl.DeviceIdType.MESH
NT = (((1,), (1,)), ((), ()))


def nt_dot(a, b):
    return lax.dot_general(a, b, NT, preferred_element_type=jnp.float32)


def square_row(rows):
    wide = rows.astype(jnp.float32)
    square = wide * wide
    high = square.astype(jnp.bfloat16)
    low = (square - high.astype(jnp.float32)).astype(jnp.bfloat16)
    ones = jnp.ones((8, rows.shape[1]), jnp.bfloat16)
    return (nt_dot(ones, high) + nt_dot(ones, low))[0:1] * (1.0 / rows.shape[1])


def spread(row):
    return jnp.broadcast_to(row, (HALF, HALF)).T


def block_sums(left, right, scale, offset_ref, start, tops, totals, row):
    inner = nt_dot(left, right)
    for c in range(CLUSTER // CHUNK):
        rows = slice(c * CHUNK, (c + 1) * CHUNK)
        offset = offset_ref[pl.ds(start + c * CHUNK, CHUNK), :]
        for half in range(CLUSTER // HALF):
            lanes = slice(half * HALF, (half + 1) * HALF)
            score = (inner[rows, lanes] + offset).reshape(CHUNK // LANES, LANES, HALF)
            top = jnp.max(score, axis=0)
            tops[pl.ds(row + c * LANES, LANES), lanes] = top
            totals[pl.ds(row + c * LANES, LANES), lanes] = jnp.sum(jnp.exp((score - top) * scale), axis=0)


def merge(tops, totals, listed):
    tops = jnp.where(listed, tops, NEG_FLOOR)
    best = jnp.max(tops, axis=0, keepdims=True)
    total = jnp.sum(jnp.where(listed, totals * jnp.exp(tops - best), 0.0), axis=0, keepdims=True)
    return best + jnp.log(total)


def kernel(groups, keys, src_hbm, tgt_hbm, sw_hbm, tw_hbm, td_hbm, pb_hbm, pc_ref, so_ref, to_ref,
           tgt_ref, sw_ref, tw_ref, td_ref, pb_ref, load_sem, gs, plse, wg, tl, acol, bcol, brow, sqt, mt, lt,
           s_send, s_recv, p_send, p_recv, w_send, w_recv, t_send, t_recv):
    g, k = lax.axis_index("group"), lax.axis_index("key")
    pos, core = k // 2, k % 2
    n_pos = keys // 2
    width = tgt_ref.shape[1]
    n_tgt = tgt_ref.shape[0] // CLUSTER
    scale = 2.0 / width / ENTROPY

    def key_peer(r):
        return lax.rem(k + r, keys)

    pairs = ((src_hbm, gs.at[k]), (sw_hbm, sw_ref), (tgt_hbm, tgt_ref), (td_hbm, td_ref),
             (pb_hbm, pb_ref), (tw_hbm, tw_ref))
    loads = [pltpu.make_async_copy(a, b, load_sem.at[n]) for n, (a, b) in enumerate(pairs)]
    for load in loads:
        load.start()

    barrier = pltpu.get_barrier_semaphore()

    def greet(r, carry):
        pl.semaphore_signal(barrier, inc=1, device_id=(g, key_peer(r)), device_id_type=MESH)
        return carry

    lax.fori_loop(1, keys, greet, 0)
    for r in range(1, groups):
        pl.semaphore_signal(barrier, inc=1, device_id=(lax.rem(g + r, groups), k), device_id_type=MESH)
    loads[0].wait()
    loads[1].wait()
    wg[k] = jnp.log(jnp.concatenate([sw_ref[0:1, :], sw_ref[1:2, :]], axis=1))
    pl.semaphore_wait(barrier, keys + groups - 2)

    def shard(slot, lane, part):
        target = (2 * (pos - 1) + core, 2 * (pos + 1) + core, 2 * pos + 1 - core)[lane]
        piece = gs.at[slot, pl.ds(pl.multiple_of(part * HALF, HALF), HALF)]
        return pltpu.make_async_remote_copy(
            src_ref=piece, dst_ref=piece, send_sem=s_send.at[lane, slot, part],
            recv_sem=s_recv.at[slot, part], device_id=(g, target), device_id_type=MESH)

    def weights(r):
        return pltpu.make_async_remote_copy(
            src_ref=wg.at[k], dst_ref=wg.at[k], send_sem=w_send.at[r], recv_sem=w_recv.at[k],
            device_id=(g, key_peer(r)), device_id_type=MESH)

    def weights_from(r):
        peer = key_peer(r)
        return pltpu.make_async_remote_copy(
            src_ref=wg.at[peer], dst_ref=wg.at[peer], send_sem=w_send.at[r], recv_sem=w_recv.at[peer],
            device_id=(g, peer), device_id_type=MESH)

    def send_own(part, carry):
        @pl.when(pos > 0)
        def _():
            shard(k, 0, part).start()

        @pl.when(pos < n_pos - 1)
        def _():
            shard(k, 1, part).start()

        shard(k, 2, part).start()
        return carry

    lax.fori_loop(0, 2, send_own, 0)

    def send_weights(r, carry):
        weights(r).start()
        return carry

    lax.fori_loop(1, keys, send_weights, 0)

    for load in loads[2:]:
        load.wait()

    def prepare(t, carry):
        sq = square_row(tgt_ref[pl.ds(pl.multiple_of(t * CLUSTER, CLUSTER), CLUSTER), :])
        sqt[pl.ds(t, 1), :] = sq
        for half in range(2):
            row = (td_ref[pl.ds(2 * t + half, 1), :] - sq[:, half * HALF : (half + 1) * HALF]) * (0.5 * width)
            acol[pl.ds(pl.multiple_of(t * CLUSTER + half * HALF, HALF), HALF), :] = spread(row)
        return carry

    lax.fori_loop(0, n_tgt, prepare, 0)

    slots = pb_ref.shape[1]
    live = lax.broadcasted_iota(jnp.int32, (1, slots), 1) < pc_ref[...]
    src_ids = jnp.where(live, pb_ref[0:1, :], -1)
    tgt_ids = pb_ref[1:2, :]

    def listed_rows(rows, row_ids, other_ids, other):
        cluster = lax.broadcasted_iota(jnp.int32, (rows * PARTS, slots), 0) // PARTS
        hit = (cluster == row_ids) & (other_ids == other)
        return jnp.sum(jnp.where(hit, 1.0, 0.0), axis=1, keepdims=True) > 0.0

    def first(slot):
        src = gs[slot]
        for t in range(n_tgt):
            block_sums(tgt_ref[t * CLUSTER : (t + 1) * CLUSTER, :], src, scale, acol, t * CLUSTER, mt, lt, t * PARTS)
        listed = listed_rows(n_tgt, tgt_ids, src_ids, slot)
        plse[k, pl.ds(slot, 1), :] = merge(mt[0 : n_tgt * PARTS, :] * scale, lt[0 : n_tgt * PARTS, :], listed)

    def stage(n, carry):
        d, part = n // 2, n % 2
        before, after = pos - d, pos + d

        @pl.when((d > 0) & (before >= 0))
        def _():
            slot = 2 * before + core
            shard(slot, 1, part).wait_recv()

            @pl.when(pos < n_pos - 1)
            def _():
                shard(slot, 1, part).start()

            shard(slot, 2, part).start()

        @pl.when((d > 0) & (after < n_pos))
        def _():
            slot = 2 * after + core
            shard(slot, 0, part).wait_recv()

            @pl.when(pos > 0)
            def _():
                shard(slot, 0, part).start()

            shard(slot, 2, part).start()

        far = d - 1 + part

        def job(forward, carry):
            at = pos + far * (2 * forward - 1)

            @pl.when((at >= 0) & (at < n_pos) & (far >= forward))
            def _():
                slot = 2 * at + core + (1 - part) * (1 - 2 * core)

                @pl.when(part == 0)
                def _():
                    shard(slot, 2, 0).wait_recv()
                    shard(slot, 2, 1).wait_recv()

                first(slot)

            return carry

        return lax.fori_loop(0, 2, job, carry)

    lax.fori_loop(1, 2 * n_pos + 1, stage, 0)

    def partial(r):
        return pltpu.make_async_remote_copy(
            src_ref=plse.at[k], dst_ref=plse.at[k], send_sem=p_send.at[r], recv_sem=p_recv.at[k],
            device_id=(g, key_peer(r)), device_id_type=MESH)

    def partial_from(r):
        peer = key_peer(r)
        return pltpu.make_async_remote_copy(
            src_ref=plse.at[peer], dst_ref=plse.at[peer], send_sem=p_send.at[r], recv_sem=p_recv.at[peer],
            device_id=(g, peer), device_id_type=MESH)

    def send_partial(r, carry):
        partial(r).start()
        return carry

    def take_partial(r, carry):
        weights_from(r).wait_recv()
        partial_from(r).wait_recv()
        return carry

    lax.fori_loop(1, keys, send_partial, 0)
    own_sq = square_row(gs[k])
    lax.fori_loop(1, keys, take_partial, 0)

    every = plse[...]
    best = jnp.max(every, axis=0)
    total = jnp.sum(jnp.exp(every - best[None]), axis=0)
    brow[...] = wg[...].reshape(keys, CLUSTER) - (best + jnp.log(total))
    own = brow[pl.ds(k, 1), :] * ENTROPY + own_sq
    so_ref[0:1, :] = own[:, :HALF]
    so_ref[1:2, :] = own[:, HALF:]

    def columns(s, carry):
        row = brow[pl.ds(s, 1), :] * (0.5 * width * ENTROPY)
        for half in range(2):
            bcol[pl.ds(pl.multiple_of(s * CLUSTER + half * HALF, HALF), HALF), :] = spread(
                row[:, half * HALF : (half + 1) * HALF])
        return carry

    lax.fori_loop(0, keys, columns, 0)

    step = math.gcd(keys, 8)

    def second(t, carry):
        tgt = tgt_ref[pl.ds(pl.multiple_of(t * CLUSTER, CLUSTER), CLUSTER), :]

        def some(c, carry):
            for j in range(step):
                s = c * step + j
                block_sums(gs[s], tgt, scale, bcol, pl.multiple_of(s * CLUSTER, CLUSTER), mt, lt,
                           pl.multiple_of(s * PARTS, PARTS))
            return carry

        lax.fori_loop(0, keys // step, some, 0)
        listed = listed_rows(keys, src_ids, tgt_ids, t)
        tl[g, pl.ds(t, 1), :] = merge(mt[0 : keys * PARTS, :] * scale, lt[0 : keys * PARTS, :], listed)
        return carry

    lax.fori_loop(0, n_tgt, second, 0, unroll=2)

    def column(r):
        return pltpu.make_async_remote_copy(
            src_ref=tl.at[g], dst_ref=tl.at[g], send_sem=t_send.at[r], recv_sem=t_recv.at[g],
            device_id=(lax.rem(g + r, groups), k), device_id_type=MESH)

    def column_from(r):
        peer = lax.rem(g + r, groups)
        return pltpu.make_async_remote_copy(
            src_ref=tl.at[peer], dst_ref=tl.at[peer], send_sem=t_send.at[r], recv_sem=t_recv.at[peer],
            device_id=(peer, k), device_id_type=MESH)

    for r in range(1, groups):
        column(r).start()

    def sent_shards(p, carry):
        slot = 2 * p + core
        for part in range(2):

            @pl.when((pos > 0) & (p >= pos))
            def _():
                shard(slot, 0, part).wait_send()

            @pl.when((pos < n_pos - 1) & (p <= pos))
            def _():
                shard(slot, 1, part).wait_send()

            shard(slot, 2, part).wait_send()
        return carry

    def sent_rows(r, carry):
        weights(r).wait_send()
        partial(r).wait_send()
        return carry

    lax.fori_loop(0, n_pos, sent_shards, 0)
    lax.fori_loop(1, keys, sent_rows, 0)
    for r in range(1, groups):
        column_from(r).wait_recv()

    every = tl[...]
    best = jnp.max(every, axis=0)
    total = jnp.sum(jnp.exp(every - best[None]), axis=0)
    lse = best + jnp.log(total)
    new = sqt[...] - lse * ENTROPY
    for t in range(n_tgt):
        for half in range(2):
            at = 2 * t + half
            to_ref[at : at + 1, :] = (
                new[t : t + 1, half * HALF : (half + 1) * HALF] + jnp.log(tw_ref[at : at + 1, :]) * ENTROPY)
    for r in range(1, groups):
        column(r).wait_send()


def local(groups, keys, src_desc, tgt_desc, src_weight, tgt_weight, tgt_dual, pair_blocks, pair_count):
    rows, width = tgt_desc.shape
    n_tgt = rows // CLUSTER
    slots = pair_blocks.shape[3]
    f32 = jnp.float32
    dma = pltpu.SemaphoreType.DMA
    most = max(keys, n_tgt)
    blocks = 2 * keys * n_tgt
    src_dual, tgt_new = pl.pallas_call(
        functools.partial(kernel, groups, keys),
        out_shape=(jax.ShapeDtypeStruct((CLUSTER // HALF, HALF), f32),
                   jax.ShapeDtypeStruct((rows // HALF, HALF), f32)),
        in_specs=[pl.BlockSpec(memory_space=pltpu.HBM)] * 6 + [pl.BlockSpec(memory_space=pltpu.VMEM)],
        out_specs=[pl.BlockSpec(memory_space=pltpu.VMEM)] * 2,
        scratch_shapes=[
            pltpu.VMEM((rows, width), jnp.bfloat16),
            pltpu.VMEM((CLUSTER // HALF, HALF), f32),
            pltpu.VMEM((rows // HALF, HALF), f32),
            pltpu.VMEM((rows // HALF, HALF), f32),
            pltpu.VMEM((2, slots), jnp.int32),
            dma((6,)),
            pltpu.VMEM((keys, CLUSTER, width), jnp.bfloat16),
            pltpu.VMEM((keys, keys, CLUSTER), f32),
            pltpu.VMEM((keys, 1, CLUSTER), f32),
            pltpu.VMEM((groups, n_tgt, CLUSTER), f32),
            pltpu.VMEM((rows, HALF), f32),
            pltpu.VMEM((keys * CLUSTER, HALF), f32),
            pltpu.VMEM((keys, CLUSTER), f32),
            pltpu.VMEM((n_tgt, CLUSTER), f32),
            pltpu.VMEM((most * PARTS, CLUSTER), f32),
            pltpu.VMEM((most * PARTS, CLUSTER), f32),
            dma((3, keys, 2)), dma((keys, 2)),
            dma((keys,)), dma((keys,)),
            dma((keys,)), dma((keys,)),
            dma((groups,)), dma((groups,)),
        ],
        compiler_params=pltpu.CompilerParams(
            collective_id=0, has_side_effects=True, vmem_limit_bytes=63 * 1024 * 1024),
        cost_estimate=pl.CostEstimate(
            flops=blocks * 2 * CLUSTER * CLUSTER * width, bytes_accessed=2 * rows * width,
            transcendentals=blocks * CLUSTER * CLUSTER),
    )(
        src_desc, tgt_desc,
        src_weight.reshape(CLUSTER // HALF, HALF),
        tgt_weight.reshape(rows // HALF, HALF),
        tgt_dual.reshape(rows // HALF, HALF),
        pair_blocks.reshape(2, slots), pair_count.reshape(1, 1),
    )
    return src_dual.reshape(CLUSTER), tgt_new.reshape(rows)


def solution(mesh):
    groups, keys = mesh.shape["group"], mesh.shape["key"]
    in_specs = (
        P(("group", "key"), None),
        P("key", None),
        P(("group", "key")),
        P("key"),
        P("key"),
        P("group", "key", None, None),
        P("group", "key"),
    )
    out_specs = (P(("group", "key")), P("key"))
    return jax.shard_map(functools.partial(local, groups, keys), mesh=mesh, in_specs=in_specs,
                         out_specs=out_specs, check_vma=False)
```

```python
import functools
import math

import jax
import jax.numpy as jnp
from jax import lax
from jax.experimental import pallas as pl
from jax.experimental.pallas import tpu as pltpu
from jax.sharding import PartitionSpec as P

CLUSTER = 256
HALF = 128
ENTROPY = 0.05
NEG_FLOOR = -1e30
LANES = 8
CHUNK = 128
PARTS = CLUSTER // CHUNK * LANES
MESH = pl.DeviceIdType.MESH
NT = (((1,), (1,)), ((), ()))


def nt_dot(a, b):
    return lax.dot_general(a, b, NT, preferred_element_type=jnp.float32)


def square_row(rows):
    wide = rows.astype(jnp.float32)
    square = wide * wide
    high = square.astype(jnp.bfloat16)
    low = (square - high.astype(jnp.float32)).astype(jnp.bfloat16)
    ones = jnp.ones((8, rows.shape[1]), jnp.bfloat16)
    return (nt_dot(ones, high) + nt_dot(ones, low))[0:1] * (1.0 / rows.shape[1])


def spread(row):
    return jnp.broadcast_to(row, (HALF, HALF)).T


def block_sums(left, right, scale, offset_ref, start, tops, totals, row):
    inner = nt_dot(left, right)
    for c in range(left.shape[0] // CHUNK):
        rows = slice(c * CHUNK, (c + 1) * CHUNK)
        offset = offset_ref[pl.ds(start + c * CHUNK, CHUNK), :]
        for half in range(CLUSTER // HALF):
            lanes = slice(half * HALF, (half + 1) * HALF)
            score = (inner[rows, lanes] + offset).reshape(CHUNK // LANES, LANES, HALF)
            top = jnp.max(score, axis=0)
            tops[pl.ds(row + c * LANES, LANES), lanes] = top
            totals[pl.ds(row + c * LANES, LANES), lanes] = jnp.sum(jnp.exp((score - top) * scale), axis=0)


def merge(tops, totals, listed):
    tops = jnp.where(listed, tops, NEG_FLOOR)
    best = jnp.max(tops, axis=0, keepdims=True)
    total = jnp.sum(jnp.where(listed, totals * jnp.exp(tops - best), 0.0), axis=0, keepdims=True)
    return best + jnp.log(total)


def kernel(groups, keys, src_hbm, tgt_hbm, sw_hbm, tw_hbm, td_hbm, pb_hbm, pc_ref, so_ref, to_ref,
           tgt_ref, sw_ref, tw_ref, td_ref, pb_ref, load_sem, gs, plse, wg, tl, acol, bcol, brow, sqt, mt, lt,
           s_send, s_recv, p_send, p_recv, w_send, w_recv, t_send, t_recv):
    g, k = lax.axis_index("group"), lax.axis_index("key")
    pos, core = k // 2, k % 2
    n_pos = keys // 2
    width = tgt_ref.shape[1]
    n_tgt = tgt_ref.shape[0] // CLUSTER
    scale = 2.0 / width / ENTROPY

    def key_peer(r):
        return lax.rem(k + r, keys)

    pairs = ((src_hbm, gs.at[k]), (sw_hbm, sw_ref), (tgt_hbm, tgt_ref), (td_hbm, td_ref),
             (pb_hbm, pb_ref), (tw_hbm, tw_ref))
    loads = [pltpu.make_async_copy(a, b, load_sem.at[n]) for n, (a, b) in enumerate(pairs)]
    for load in loads:
        load.start()

    barrier = pltpu.get_barrier_semaphore()

    def greet(r, carry):
        pl.semaphore_signal(barrier, inc=1, device_id=(g, key_peer(r)), device_id_type=MESH)
        return carry

    lax.fori_loop(1, keys, greet, 0)
    for r in range(1, groups):
        pl.semaphore_signal(barrier, inc=1, device_id=(lax.rem(g + r, groups), k), device_id_type=MESH)
    loads[0].wait()
    loads[1].wait()
    wg[k] = jnp.log(jnp.concatenate([sw_ref[0:1, :], sw_ref[1:2, :]], axis=1))
    pl.semaphore_wait(barrier, keys + groups - 2)

    def shard(slot, lane, part):
        target = (2 * (pos - 1) + core, 2 * (pos + 1) + core, 2 * pos + 1 - core)[lane]
        piece = gs.at[slot, pl.ds(pl.multiple_of(part * HALF, HALF), HALF)]
        return pltpu.make_async_remote_copy(
            src_ref=piece, dst_ref=piece, send_sem=s_send.at[lane, slot, part],
            recv_sem=s_recv.at[slot, part], device_id=(g, target), device_id_type=MESH)

    def weights(r):
        return pltpu.make_async_remote_copy(
            src_ref=wg.at[k], dst_ref=wg.at[k], send_sem=w_send.at[r], recv_sem=w_recv.at[k],
            device_id=(g, key_peer(r)), device_id_type=MESH)

    def weights_from(r):
        peer = key_peer(r)
        return pltpu.make_async_remote_copy(
            src_ref=wg.at[peer], dst_ref=wg.at[peer], send_sem=w_send.at[r], recv_sem=w_recv.at[peer],
            device_id=(g, peer), device_id_type=MESH)

    def send_own(part, carry):
        @pl.when(pos > 0)
        def _():
            shard(k, 0, part).start()

        @pl.when(pos < n_pos - 1)
        def _():
            shard(k, 1, part).start()

        shard(k, 2, part).start()
        return carry

    lax.fori_loop(0, 2, send_own, 0)

    def send_weights(r, carry):
        weights(r).start()
        return carry

    lax.fori_loop(1, keys, send_weights, 0)

    for load in loads[2:]:
        load.wait()

    def prepare(t, carry):
        sq = square_row(tgt_ref[pl.ds(pl.multiple_of(t * CLUSTER, CLUSTER), CLUSTER), :])
        sqt[pl.ds(t, 1), :] = sq
        for half in range(2):
            row = (td_ref[pl.ds(2 * t + half, 1), :] - sq[:, half * HALF : (half + 1) * HALF]) * (0.5 * width)
            acol[pl.ds(pl.multiple_of(t * CLUSTER + half * HALF, HALF), HALF), :] = spread(row)
        return carry

    lax.fori_loop(0, n_tgt, prepare, 0)

    slots = pb_ref.shape[1]
    live = lax.broadcasted_iota(jnp.int32, (1, slots), 1) < pc_ref[...]
    src_ids = jnp.where(live, pb_ref[0:1, :], -1)
    tgt_ids = pb_ref[1:2, :]

    def listed_rows(rows, row_ids, other_ids, other):
        cluster = lax.broadcasted_iota(jnp.int32, (rows * PARTS, slots), 0) // PARTS
        hit = (cluster == row_ids) & (other_ids == other)
        return jnp.sum(jnp.where(hit, 1.0, 0.0), axis=1, keepdims=True) > 0.0

    def first(slot):
        src = gs[slot]
        block_sums(tgt_ref[...], src, scale, acol, 0, mt, lt, 0)
        listed = listed_rows(n_tgt, tgt_ids, src_ids, slot)
        plse[k, pl.ds(slot, 1), :] = merge(mt[0 : n_tgt * PARTS, :] * scale, lt[0 : n_tgt * PARTS, :], listed)

    def stage(n, carry):
        d, part = n // 2, n % 2
        before, after = pos - d, pos + d

        @pl.when((d > 0) & (before >= 0))
        def _():
            slot = 2 * before + core
            shard(slot, 1, part).wait_recv()

            @pl.when(pos < n_pos - 1)
            def _():
                shard(slot, 1, part).start()

            shard(slot, 2, part).start()

        @pl.when((d > 0) & (after < n_pos))
        def _():
            slot = 2 * after + core
            shard(slot, 0, part).wait_recv()

            @pl.when(pos > 0)
            def _():
                shard(slot, 0, part).start()

            shard(slot, 2, part).start()

        far = d - 1 + part

        def job(forward, carry):
            at = pos + far * (2 * forward - 1)

            @pl.when((at >= 0) & (at < n_pos) & (far >= forward))
            def _():
                slot = 2 * at + core + (1 - part) * (1 - 2 * core)

                @pl.when(part == 0)
                def _():
                    shard(slot, 2, 0).wait_recv()
                    shard(slot, 2, 1).wait_recv()

                first(slot)

            return carry

        return lax.fori_loop(0, 2, job, carry)

    lax.fori_loop(1, 2 * n_pos + 1, stage, 0)

    def partial(r):
        return pltpu.make_async_remote_copy(
            src_ref=plse.at[k], dst_ref=plse.at[k], send_sem=p_send.at[r], recv_sem=p_recv.at[k],
            device_id=(g, key_peer(r)), device_id_type=MESH)

    def partial_from(r):
        peer = key_peer(r)
        return pltpu.make_async_remote_copy(
            src_ref=plse.at[peer], dst_ref=plse.at[peer], send_sem=p_send.at[r], recv_sem=p_recv.at[peer],
            device_id=(g, peer), device_id_type=MESH)

    def send_partial(r, carry):
        partial(r).start()
        return carry

    def take_partial(r, carry):
        weights_from(r).wait_recv()
        partial_from(r).wait_recv()
        return carry

    lax.fori_loop(1, keys, send_partial, 0)
    own_sq = square_row(gs[k])
    lax.fori_loop(1, keys, take_partial, 0)

    every = plse[...]
    best = jnp.max(every, axis=0)
    total = jnp.sum(jnp.exp(every - best[None]), axis=0)
    brow[...] = wg[...].reshape(keys, CLUSTER) - (best + jnp.log(total))
    own = brow[pl.ds(k, 1), :] * ENTROPY + own_sq
    so_ref[0:1, :] = own[:, :HALF]
    so_ref[1:2, :] = own[:, HALF:]

    def columns(s, carry):
        row = brow[pl.ds(s, 1), :] * (0.5 * width * ENTROPY)
        for half in range(2):
            bcol[pl.ds(pl.multiple_of(s * CLUSTER + half * HALF, HALF), HALF), :] = spread(
                row[:, half * HALF : (half + 1) * HALF])
        return carry

    lax.fori_loop(0, keys, columns, 0)

    step = math.gcd(keys, 8)

    def second(t, carry):
        tgt = tgt_ref[pl.ds(pl.multiple_of(t * CLUSTER, CLUSTER), CLUSTER), :]

        def some(c, carry):
            some_src = gs[pl.ds(c * step, step)].reshape(step * CLUSTER, width)
            block_sums(some_src, tgt, scale, bcol, pl.multiple_of(c * step * CLUSTER, CLUSTER), mt, lt,
                       pl.multiple_of(c * step * PARTS, PARTS))
            return carry

        lax.fori_loop(0, keys // step, some, 0)
        listed = listed_rows(keys, src_ids, tgt_ids, t)
        tl[g, pl.ds(t, 1), :] = merge(mt[0 : keys * PARTS, :] * scale, lt[0 : keys * PARTS, :], listed)
        return carry

    lax.fori_loop(0, n_tgt, second, 0, unroll=2)

    def column(r):
        return pltpu.make_async_remote_copy(
            src_ref=tl.at[g], dst_ref=tl.at[g], send_sem=t_send.at[r], recv_sem=t_recv.at[g],
            device_id=(lax.rem(g + r, groups), k), device_id_type=MESH)

    def column_from(r):
        peer = lax.rem(g + r, groups)
        return pltpu.make_async_remote_copy(
            src_ref=tl.at[peer], dst_ref=tl.at[peer], send_sem=t_send.at[r], recv_sem=t_recv.at[peer],
            device_id=(peer, k), device_id_type=MESH)

    for r in range(1, groups):
        column(r).start()

    def sent_shards(p, carry):
        slot = 2 * p + core
        for part in range(2):

            @pl.when((pos > 0) & (p >= pos))
            def _():
                shard(slot, 0, part).wait_send()

            @pl.when((pos < n_pos - 1) & (p <= pos))
            def _():
                shard(slot, 1, part).wait_send()

            shard(slot, 2, part).wait_send()
        return carry

    def sent_rows(r, carry):
        weights(r).wait_send()
        partial(r).wait_send()
        return carry

    lax.fori_loop(0, n_pos, sent_shards, 0)
    lax.fori_loop(1, keys, sent_rows, 0)
    for r in range(1, groups):
        column_from(r).wait_recv()

    every = tl[...]
    best = jnp.max(every, axis=0)
    total = jnp.sum(jnp.exp(every - best[None]), axis=0)
    lse = best + jnp.log(total)
    new = sqt[...] - lse * ENTROPY
    for t in range(n_tgt):
        for half in range(2):
            at = 2 * t + half
            to_ref[at : at + 1, :] = (
                new[t : t + 1, half * HALF : (half + 1) * HALF] + jnp.log(tw_ref[at : at + 1, :]) * ENTROPY)
    for r in range(1, groups):
        column(r).wait_send()


def local(groups, keys, src_desc, tgt_desc, src_weight, tgt_weight, tgt_dual, pair_blocks, pair_count):
    rows, width = tgt_desc.shape
    n_tgt = rows // CLUSTER
    slots = pair_blocks.shape[3]
    f32 = jnp.float32
    dma = pltpu.SemaphoreType.DMA
    most = max(keys, n_tgt)
    blocks = 2 * keys * n_tgt
    src_dual, tgt_new = pl.pallas_call(
        functools.partial(kernel, groups, keys),
        out_shape=(jax.ShapeDtypeStruct((CLUSTER // HALF, HALF), f32),
                   jax.ShapeDtypeStruct((rows // HALF, HALF), f32)),
        in_specs=[pl.BlockSpec(memory_space=pltpu.HBM)] * 6 + [pl.BlockSpec(memory_space=pltpu.VMEM)],
        out_specs=[pl.BlockSpec(memory_space=pltpu.VMEM)] * 2,
        scratch_shapes=[
            pltpu.VMEM((rows, width), jnp.bfloat16),
            pltpu.VMEM((CLUSTER // HALF, HALF), f32),
            pltpu.VMEM((rows // HALF, HALF), f32),
            pltpu.VMEM((rows // HALF, HALF), f32),
            pltpu.VMEM((2, slots), jnp.int32),
            dma((6,)),
            pltpu.VMEM((keys, CLUSTER, width), jnp.bfloat16),
            pltpu.VMEM((keys, keys, CLUSTER), f32),
            pltpu.VMEM((keys, 1, CLUSTER), f32),
            pltpu.VMEM((groups, n_tgt, CLUSTER), f32),
            pltpu.VMEM((rows, HALF), f32),
            pltpu.VMEM((keys * CLUSTER, HALF), f32),
            pltpu.VMEM((keys, CLUSTER), f32),
            pltpu.VMEM((n_tgt, CLUSTER), f32),
            pltpu.VMEM((most * PARTS, CLUSTER), f32),
            pltpu.VMEM((most * PARTS, CLUSTER), f32),
            dma((3, keys, 2)), dma((keys, 2)),
            dma((keys,)), dma((keys,)),
            dma((keys,)), dma((keys,)),
            dma((groups,)), dma((groups,)),
        ],
        compiler_params=pltpu.CompilerParams(
            collective_id=0, has_side_effects=True, vmem_limit_bytes=63 * 1024 * 1024),
        cost_estimate=pl.CostEstimate(
            flops=blocks * 2 * CLUSTER * CLUSTER * width, bytes_accessed=2 * rows * width,
            transcendentals=blocks * CLUSTER * CLUSTER),
    )(
        src_desc, tgt_desc,
        src_weight.reshape(CLUSTER // HALF, HALF),
        tgt_weight.reshape(rows // HALF, HALF),
        tgt_dual.reshape(rows // HALF, HALF),
        pair_blocks.reshape(2, slots), pair_count.reshape(1, 1),
    )
    return src_dual.reshape(CLUSTER), tgt_new.reshape(rows)


def solution(mesh):
    groups, keys = mesh.shape["group"], mesh.shape["key"]
    in_specs = (
        P(("group", "key"), None),
        P("key", None),
        P(("group", "key")),
        P("key"),
        P("key"),
        P("group", "key", None, None),
        P("group", "key"),
    )
    out_specs = (P(("group", "key")), P("key"))
    return jax.shard_map(functools.partial(local, groups, keys), mesh=mesh, in_specs=in_specs,
                         out_specs=out_specs, check_vma=False)
```

```python
import functools
import math

import jax
import jax.numpy as jnp
from jax import lax
from jax.experimental import pallas as pl
from jax.experimental.pallas import tpu as pltpu
from jax.sharding import PartitionSpec as P

CLUSTER = 256
HALF = 128
ENTROPY = 0.05
NEG_FLOOR = -1e30
LANES = 8
CHUNK = 128
PARTS = CLUSTER // CHUNK * LANES
MESH = pl.DeviceIdType.MESH
NT = (((1,), (1,)), ((), ()))


def nt_dot(a, b):
    return lax.dot_general(a, b, NT, preferred_element_type=jnp.float32)


def square_row(rows):
    wide = rows.astype(jnp.float32)
    square = wide * wide
    high = square.astype(jnp.bfloat16)
    low = (square - high.astype(jnp.float32)).astype(jnp.bfloat16)
    ones = jnp.ones((8, rows.shape[1]), jnp.bfloat16)
    return (nt_dot(ones, high) + nt_dot(ones, low))[0:1] * (1.0 / rows.shape[1])


def spread(row):
    return jnp.broadcast_to(row, (HALF, HALF)).T


def block_sums(left, right, scale, offset_ref, start, tops, totals, row):
    inner = nt_dot(left, right)
    for c in range(left.shape[0] // CHUNK):
        rows = slice(c * CHUNK, (c + 1) * CHUNK)
        offset = offset_ref[pl.ds(start + c * CHUNK, CHUNK), :]
        for half in range(CLUSTER // HALF):
            lanes = slice(half * HALF, (half + 1) * HALF)
            score = (inner[rows, lanes] + offset).reshape(CHUNK // LANES, LANES, HALF)
            top = jnp.max(score, axis=0)
            tops[pl.ds(row + c * LANES, LANES), lanes] = top
            totals[pl.ds(row + c * LANES, LANES), lanes] = jnp.sum(jnp.exp((score - top) * scale), axis=0)


def merge(tops, totals, listed):
    tops = jnp.where(listed, tops, NEG_FLOOR)
    best = jnp.max(tops, axis=0, keepdims=True)
    total = jnp.sum(jnp.where(listed, totals * jnp.exp(tops - best), 0.0), axis=0, keepdims=True)
    return best + jnp.log(total)


def kernel(groups, keys, src_hbm, tgt_hbm, sw_hbm, tw_hbm, td_hbm, pb_hbm, pc_ref, so_ref, to_ref,
           tgt_ref, sw_ref, tw_ref, td_ref, pb_ref, load_sem, gs, plse, wg, tl, acol, bcol, brow, sqt, mt, lt,
           s_send, s_recv, p_send, p_recv, w_send, w_recv, t_send, t_recv):
    g, k = lax.axis_index("group"), lax.axis_index("key")
    pos, core = k // 2, k % 2
    n_pos = keys // 2
    width = tgt_ref.shape[1]
    n_tgt = tgt_ref.shape[0] // CLUSTER
    scale = 2.0 / width / ENTROPY

    def key_peer(r):
        return lax.rem(k + r, keys)

    pairs = ((src_hbm, gs.at[k]), (sw_hbm, sw_ref), (tgt_hbm, tgt_ref), (td_hbm, td_ref),
             (pb_hbm, pb_ref), (tw_hbm, tw_ref))
    loads = [pltpu.make_async_copy(a, b, load_sem.at[n]) for n, (a, b) in enumerate(pairs)]
    for load in loads:
        load.start()

    barrier = pltpu.get_barrier_semaphore()

    def greet(r, carry):
        pl.semaphore_signal(barrier, inc=1, device_id=(g, key_peer(r)), device_id_type=MESH)
        return carry

    lax.fori_loop(1, keys, greet, 0)
    for r in range(1, groups):
        pl.semaphore_signal(barrier, inc=1, device_id=(lax.rem(g + r, groups), k), device_id_type=MESH)
    loads[0].wait()
    loads[1].wait()
    wg[k] = jnp.log(jnp.concatenate([sw_ref[0:1, :], sw_ref[1:2, :]], axis=1))
    pl.semaphore_wait(barrier, keys + groups - 2)

    def shard(slot, lane, part):
        target = (2 * (pos - 1) + core, 2 * (pos + 1) + core, 2 * pos + 1 - core)[lane]
        piece = gs.at[slot, pl.ds(pl.multiple_of(part * HALF, HALF), HALF)]
        return pltpu.make_async_remote_copy(
            src_ref=piece, dst_ref=piece, send_sem=s_send.at[lane, slot, part],
            recv_sem=s_recv.at[slot, part], device_id=(g, target), device_id_type=MESH)

    def weights(r):
        return pltpu.make_async_remote_copy(
            src_ref=wg.at[k], dst_ref=wg.at[k], send_sem=w_send.at[r], recv_sem=w_recv.at[k],
            device_id=(g, key_peer(r)), device_id_type=MESH)

    def send_own(part, carry):
        @pl.when(pos > 0)
        def _():
            shard(k, 0, part).start()

        @pl.when(pos < n_pos - 1)
        def _():
            shard(k, 1, part).start()

        shard(k, 2, part).start()
        return carry

    lax.fori_loop(0, 2, send_own, 0)

    def send_weights(r, carry):
        weights(r).start()
        return carry

    lax.fori_loop(1, keys, send_weights, 0)

    for load in loads[2:]:
        load.wait()

    def prepare(t, carry):
        sq = square_row(tgt_ref[pl.ds(pl.multiple_of(t * CLUSTER, CLUSTER), CLUSTER), :])
        sqt[pl.ds(t, 1), :] = sq
        for half in range(2):
            row = (td_ref[pl.ds(2 * t + half, 1), :] - sq[:, half * HALF : (half + 1) * HALF]) * (0.5 * width)
            acol[pl.ds(pl.multiple_of(t * CLUSTER + half * HALF, HALF), HALF), :] = spread(row)
        return carry

    lax.fori_loop(0, n_tgt, prepare, 0)

    slots = pb_ref.shape[1]
    live = lax.broadcasted_iota(jnp.int32, (1, slots), 1) < pc_ref[...]
    src_ids = jnp.where(live, pb_ref[0:1, :], -1)
    tgt_ids = pb_ref[1:2, :]

    def listed_rows(rows, row_ids, other_ids, other):
        cluster = lax.broadcasted_iota(jnp.int32, (rows * PARTS, slots), 0) // PARTS
        hit = (cluster == row_ids) & (other_ids == other)
        return jnp.sum(jnp.where(hit, 1.0, 0.0), axis=1, keepdims=True) > 0.0

    def first(slot):
        src = gs[slot]
        block_sums(tgt_ref[...], src, scale, acol, 0, mt, lt, 0)
        listed = listed_rows(n_tgt, tgt_ids, src_ids, slot)
        plse[k, slot] = merge(mt[0 : n_tgt * PARTS, :] * scale, lt[0 : n_tgt * PARTS, :], listed)

    spans = ((2, keys - 4), (0, 2), (keys - 2, 2))

    def partial(span, sender, r):
        low, count = spans[span]
        piece = plse.at[sender, pl.ds(low, count)]
        return pltpu.make_async_remote_copy(
            src_ref=piece, dst_ref=piece, send_sem=p_send.at[span, r], recv_sem=p_recv.at[span, sender],
            device_id=(g, key_peer(r)), device_id_type=MESH)

    inner_far = jnp.maximum(jnp.abs(pos - 1), jnp.abs(n_pos - 2 - pos))

    def stage(n, carry):
        d, part = n // 2, n % 2
        before, after = pos - d, pos + d

        @pl.when((d > 0) & (before >= 0))
        def _():
            slot = 2 * before + core
            shard(slot, 1, part).wait_recv()

            @pl.when(pos < n_pos - 1)
            def _():
                shard(slot, 1, part).start()

            shard(slot, 2, part).start()

        @pl.when((d > 0) & (after < n_pos))
        def _():
            slot = 2 * after + core
            shard(slot, 0, part).wait_recv()

            @pl.when(pos > 0)
            def _():
                shard(slot, 0, part).start()

            shard(slot, 2, part).start()

        far = d - 1 + part

        def job(forward, carry):
            at = pos + far * (2 * forward - 1)

            @pl.when((at >= 0) & (at < n_pos) & (far >= forward))
            def _():
                slot = 2 * at + core + (1 - part) * (1 - 2 * core)

                @pl.when(part == 0)
                def _():
                    shard(slot, 2, 0).wait_recv()
                    shard(slot, 2, 1).wait_recv()

                first(slot)

            return carry

        lax.fori_loop(0, 2, job, 0)

        @pl.when(n == 2 * (inner_far + 1))
        def _():
            def send_inner(r, carry):
                partial(0, k, r).start()
                return carry

            lax.fori_loop(1, keys, send_inner, 0)

        return carry

    lax.fori_loop(1, 2 * n_pos + 1, stage, 0)

    def send_outer(r, carry):
        partial(1, k, r).start()
        partial(2, k, r).start()
        return carry

    lax.fori_loop(1, keys, send_outer, 0)

    def potentials(span):
        low, count = spans[span]

        def potential(s, carry):
            every = plse[:, s]
            best = jnp.max(every, axis=0)
            row = wg[s] - (best + jnp.log(jnp.sum(jnp.exp(every - best[None]), axis=0)))
            brow[s] = row
            row = row * (0.5 * width * ENTROPY)
            for half in range(2):
                bcol[pl.ds(pl.multiple_of(s * CLUSTER + half * HALF, HALF), HALF), :] = spread(
                    row[:, half * HALF : (half + 1) * HALF])
            return carry

        lax.fori_loop(low, low + count, potential, 0, unroll=2)

    def sweep(span):
        low, count = spans[span]
        step = math.gcd(count, 4)

        def second(t, carry):
            tgt = tgt_ref[pl.ds(pl.multiple_of(t * CLUSTER, CLUSTER), CLUSTER), :]

            def some(c, carry):
                s = low + c * step
                some_src = gs[pl.ds(s, step)].reshape(step * CLUSTER, width)
                block_sums(some_src, tgt, scale, bcol, pl.multiple_of(s * CLUSTER, CLUSTER), mt, lt,
                           pl.multiple_of((t * keys + s) * PARTS, PARTS))
                return carry

            return lax.fori_loop(0, count // step, some, carry)

        lax.fori_loop(0, n_tgt, second, 0, unroll=2)

    own_sq = square_row(gs[k])

    def take_inner(r, carry):
        pltpu.make_async_remote_copy(
            src_ref=wg.at[key_peer(r)], dst_ref=wg.at[key_peer(r)], send_sem=w_send.at[r],
            recv_sem=w_recv.at[key_peer(r)], device_id=(g, key_peer(r)), device_id_type=MESH).wait_recv()
        partial(0, key_peer(r), r).wait_recv()
        return carry

    lax.fori_loop(1, keys, take_inner, 0)
    potentials(0)
    sweep(0)

    def take_outer(r, carry):
        partial(1, key_peer(r), r).wait_recv()
        partial(2, key_peer(r), r).wait_recv()
        return carry

    lax.fori_loop(1, keys, take_outer, 0)
    for span in (1, 2):
        potentials(span)
        sweep(span)
    own = brow[k] * ENTROPY + own_sq
    so_ref[0:1, :] = own[:, :HALF]
    so_ref[1:2, :] = own[:, HALF:]

    def columns(t, carry):
        listed = listed_rows(keys, src_ids, tgt_ids, t)
        rows = pl.ds(pl.multiple_of(t * keys * PARTS, PARTS), keys * PARTS)
        tl[g, pl.ds(t, 1), :] = merge(mt[rows, :] * scale, lt[rows, :], listed)
        return carry

    lax.fori_loop(0, n_tgt, columns, 0, unroll=2)

    def column(r):
        return pltpu.make_async_remote_copy(
            src_ref=tl.at[g], dst_ref=tl.at[g], send_sem=t_send.at[r], recv_sem=t_recv.at[g],
            device_id=(lax.rem(g + r, groups), k), device_id_type=MESH)

    def column_from(r):
        peer = lax.rem(g + r, groups)
        return pltpu.make_async_remote_copy(
            src_ref=tl.at[peer], dst_ref=tl.at[peer], send_sem=t_send.at[r], recv_sem=t_recv.at[peer],
            device_id=(peer, k), device_id_type=MESH)

    for r in range(1, groups):
        column(r).start()

    def sent_shards(p, carry):
        slot = 2 * p + core
        for part in range(2):

            @pl.when((pos > 0) & (p >= pos))
            def _():
                shard(slot, 0, part).wait_send()

            @pl.when((pos < n_pos - 1) & (p <= pos))
            def _():
                shard(slot, 1, part).wait_send()

            shard(slot, 2, part).wait_send()
        return carry

    def sent_rows(r, carry):
        weights(r).wait_send()
        for span in range(3):
            partial(span, k, r).wait_send()
        return carry

    lax.fori_loop(0, n_pos, sent_shards, 0)
    lax.fori_loop(1, keys, sent_rows, 0)
    for r in range(1, groups):
        column_from(r).wait_recv()

    every = tl[...]
    best = jnp.max(every, axis=0)
    total = jnp.sum(jnp.exp(every - best[None]), axis=0)
    lse = best + jnp.log(total)
    new = sqt[...] - lse * ENTROPY
    for t in range(n_tgt):
        for half in range(2):
            at = 2 * t + half
            to_ref[at : at + 1, :] = (
                new[t : t + 1, half * HALF : (half + 1) * HALF] + jnp.log(tw_ref[at : at + 1, :]) * ENTROPY)
    for r in range(1, groups):
        column(r).wait_send()


def local(groups, keys, src_desc, tgt_desc, src_weight, tgt_weight, tgt_dual, pair_blocks, pair_count):
    rows, width = tgt_desc.shape
    n_tgt = rows // CLUSTER
    slots = pair_blocks.shape[3]
    f32 = jnp.float32
    dma = pltpu.SemaphoreType.DMA
    blocks = 2 * keys * n_tgt
    src_dual, tgt_new = pl.pallas_call(
        functools.partial(kernel, groups, keys),
        out_shape=(jax.ShapeDtypeStruct((CLUSTER // HALF, HALF), f32),
                   jax.ShapeDtypeStruct((rows // HALF, HALF), f32)),
        in_specs=[pl.BlockSpec(memory_space=pltpu.HBM)] * 6 + [pl.BlockSpec(memory_space=pltpu.VMEM)],
        out_specs=[pl.BlockSpec(memory_space=pltpu.VMEM)] * 2,
        scratch_shapes=[
            pltpu.VMEM((rows, width), jnp.bfloat16),
            pltpu.VMEM((CLUSTER // HALF, HALF), f32),
            pltpu.VMEM((rows // HALF, HALF), f32),
            pltpu.VMEM((rows // HALF, HALF), f32),
            pltpu.VMEM((2, slots), jnp.int32),
            dma((6,)),
            pltpu.VMEM((keys, CLUSTER, width), jnp.bfloat16),
            pltpu.VMEM((keys, keys, 1, CLUSTER), f32),
            pltpu.VMEM((keys, 1, CLUSTER), f32),
            pltpu.VMEM((groups, n_tgt, CLUSTER), f32),
            pltpu.VMEM((rows, HALF), f32),
            pltpu.VMEM((keys * CLUSTER, HALF), f32),
            pltpu.VMEM((keys, 1, CLUSTER), f32),
            pltpu.VMEM((n_tgt, CLUSTER), f32),
            pltpu.VMEM((n_tgt * keys * PARTS, CLUSTER), f32),
            pltpu.VMEM((n_tgt * keys * PARTS, CLUSTER), f32),
            dma((3, keys, 2)), dma((keys, 2)),
            dma((3, keys)), dma((3, keys)),
            dma((keys,)), dma((keys,)),
            dma((groups,)), dma((groups,)),
        ],
        compiler_params=pltpu.CompilerParams(
            collective_id=0, has_side_effects=True, vmem_limit_bytes=63 * 1024 * 1024),
        cost_estimate=pl.CostEstimate(
            flops=blocks * 2 * CLUSTER * CLUSTER * width, bytes_accessed=2 * rows * width,
            transcendentals=blocks * CLUSTER * CLUSTER),
    )(
        src_desc, tgt_desc,
        src_weight.reshape(CLUSTER // HALF, HALF),
        tgt_weight.reshape(rows // HALF, HALF),
        tgt_dual.reshape(rows // HALF, HALF),
        pair_blocks.reshape(2, slots), pair_count.reshape(1, 1),
    )
    return src_dual.reshape(CLUSTER), tgt_new.reshape(rows)


def solution(mesh):
    groups, keys = mesh.shape["group"], mesh.shape["key"]
    in_specs = (
        P(("group", "key"), None),
        P("key", None),
        P(("group", "key")),
        P("key"),
        P("key"),
        P("group", "key", None, None),
        P("group", "key"),
    )
    out_specs = (P(("group", "key")), P("key"))
    return jax.shard_map(functools.partial(local, groups, keys), mesh=mesh, in_specs=in_specs,
                         out_specs=out_specs, check_vma=False)
```
